32 devices in a mesh: dom: 16 (over z, y, x), seed: 2 (over core).
Axes of the slice: x: 2, y: 2, z: 4, core: 2. Of those that a mesh axis runs over, the one named last changes fastest.
Arguments:
- rank_in: float32 [128, 262144], P('seed', 'dom'), as said below
- band_tiles: bfloat16 [2048, 3, 128, 128], P('dom'), as said below
- off_tiles: bfloat16 [8192, 128, 128], P('dom'), as said below
- tile_src: int32 [16, 512], P('dom'), may hold values from 0 to 2047, as said below
- tile_row: int32 [16, 512], P('dom'), may hold values from 0 to 127
- tile_count: int32 [16], P('dom'), may hold values from 256 to 512, as said below
- seed_ids: int32 [128], P('seed'), may hold values from 0 to 262143
- dangling: int32 [262144], P('dom'), may hold values 0 or 1
Outputs:
- rank_out: float32 [128, 262144], P('seed', 'dom')
- change: float32 [3, 128], P(None, 'seed')
- total_change: float32 [3], replicated
- seed_score: float32 [128], P('seed')
The draws below stay inside these ranges and needn't reach their ends.
Inputs may be any that keep to these rules, and one draw needn't show every extreme that they name: `rank_in`: positive. `band_tiles`: nonnegative transition weights. `off_tiles`: nonnegative transition weights. `tile_src`: every source block is held by another index of dom than the tile; the live tiles of one index of dom read at most 2 distinct blocks held by any one other index. The first tile_count[g] slots of index g are live, the rest are padding.
All inputs are finite; a program needn't handle non-finite values. No bound on the sum of `dangling` on one device may be relied on, other than what follows from the above.
Results may differ from the reference program's by a relative error of at most 0.0003.
Values may be sent and summed in bfloat16 or wider, within the bound.
A program may use at most 192 MiB of HBM per device.

```python
import math
import jax
import jax.numpy as jnp
from jax import lax

S = 128
BLK = 128
NB_DEV = 128
CAP = 2
ITERS = 3
KT = 512
TILES = 8192
NBLK = 2048
NV = 262144
N_DOM = 16


def pick_device(key):
    return jax.random.randint(jax.random.fold_in(key, 7), (), 0, N_DOM)


def draw_tile_count(key, part):
    counts = jax.random.randint(jax.random.fold_in(key, 11), (N_DOM,), KT // 2, KT + 1)
    chosen = pick_device(key)
    return jnp.where(jnp.arange(N_DOM) == chosen, KT, counts).astype(jnp.int32)


def draw_tile_src(key, part):
    step_key = jax.random.fold_in(key, 21)
    offset_key = jax.random.fold_in(key, 22)
    within_key = jax.random.fold_in(key, 23)
    device = jnp.arange(N_DOM, dtype=jnp.int32)[:, None]
    slots = jnp.arange(KT, dtype=jnp.int32)[None, :]
    stride = jax.random.randint(step_key, (N_DOM, KT), 1, N_DOM)
    holder = (device + stride) % N_DOM
    offset = jax.random.randint(offset_key, (N_DOM, N_DOM), 0, NB_DEV)
    within = jax.random.randint(within_key, (N_DOM, KT), 0, CAP)
    chosen = pick_device(key)
    forced = jnp.logical_and(device == chosen, slots < CAP * (N_DOM - 1))
    holder = jnp.where(forced, (chosen + 1 + slots // CAP) % N_DOM, holder)
    within = jnp.where(forced, slots % CAP, within)
    start = jnp.take_along_axis(offset, holder, axis=1)
    inside = (start + within) % NB_DEV
    return (holder * NB_DEV + inside).astype(jnp.int32)


def sparse_tiles(key, shape):
    keep = (jax.random.uniform(jax.random.fold_in(key, 31), shape) < 0.25).astype(jnp.float32)
    value_key = jax.random.fold_in(key, 32)
    values = jnp.exp(jax.random.uniform(value_key, shape, jnp.float32, math.log(0.1), math.log(10.0)))
    scale = 1.0 / (0.54 * BLK * (3.0 + KT / NB_DEV))
    return (keep * values * scale).astype(jnp.bfloat16)


def draw_band_tiles(key, part):
    return sparse_tiles(key, (NBLK, 3, BLK, BLK))


def draw_off_tiles(key, part):
    return sparse_tiles(jax.random.fold_in(key, 5), (TILES, BLK, BLK))


def draw_rank_in(key, part):
    row_scale = jnp.exp(jax.random.uniform(jax.random.fold_in(key, 41), (1, NV), jnp.float32, math.log(0.3), math.log(3.0)))
    col_scale = jnp.exp(jax.random.uniform(jax.random.fold_in(key, 42), (S, 1), jnp.float32, math.log(0.5), math.log(2.0)))
    rising = 1.0 + 2.0 * jnp.arange(NV, dtype=jnp.float32)[None, :] / NV
    entry_key = jax.random.fold_in(key, 43)
    entry = jnp.exp(jax.random.uniform(entry_key, (S, NV), jnp.float32, math.log(0.5), math.log(2.0)))
    return row_scale * col_scale * entry * rising


def with_ends(drawn, rng, low, high):
    longest = drawn.shape.index(max(drawn.shape))
    spots = []
    for shift in (0, 1):
        where = [jax.random.randint(jax.random.fold_in(rng, axis), (), 0, length) for axis, length in enumerate(drawn.shape)]
        where[longest] = (where[longest] + shift) % drawn.shape[longest]
        spots.append(tuple(where))
    return drawn.at[spots[0]].set(low).at[spots[1]].set(high)


def setup_inputs(seed: int = 0) -> dict:
    keys = jax.random.split(jax.random.key(seed), 9)
    return {
        "rank_in": draw_rank_in(jax.random.fold_in(keys[8], 71), 0),
        "band_tiles": draw_band_tiles(jax.random.fold_in(keys[8], 71), 0),
        "off_tiles": draw_off_tiles(jax.random.fold_in(keys[8], 71), 0),
        "tile_src": draw_tile_src(jax.random.fold_in(keys[8], 71), 0),
        "tile_row": with_ends(jax.random.randint(keys[4], (N_DOM, KT), 0, NB_DEV), jax.random.fold_in(keys[4], 1), 0, NB_DEV - 1).astype(jnp.int32),
        "tile_count": draw_tile_count(jax.random.fold_in(keys[8], 71), 0),
        "seed_ids": with_ends(jax.random.randint(keys[6], (S,), 0, NV), jax.random.fold_in(keys[6], 1), 0, NV - 1).astype(jnp.int32),
        "dangling": with_ends((jax.random.randint(keys[7], (NV,), 0, 4) < 1).astype(jnp.int32), jax.random.fold_in(keys[7], 1), 0, 1),
    }


DAMP = 0.85


def reference(rank_in, band_tiles, off_tiles, tile_src, tile_row, tile_count, seed_ids, dangling):
    dead_ends = dangling.astype(jnp.float32)
    keep_share = 1.0 - dead_ends
    vertices = jnp.arange(NV, dtype=jnp.int32)
    live_slots = (jnp.arange(KT, dtype=jnp.int32)[None, :] < tile_count[:, None]).reshape(-1)
    targets = (jnp.arange(N_DOM, dtype=jnp.int32)[:, None] * NB_DEV + tile_row).reshape(-1)
    targets = jnp.where(live_slots, targets, NBLK).astype(jnp.int32)
    sources = tile_src.reshape(-1).astype(jnp.int32)
    band_wide = band_tiles.astype(jnp.float32)
    off_wide = off_tiles.astype(jnp.float32)
    highest = lax.Precision.HIGHEST

    def one_group(packed):
        rank_now, seed_group = packed
        seed_mask = (seed_group[:, None] == vertices[None, :]).astype(jnp.float32)
        restart = (1.0 - DAMP) * seed_mask
        changes = []
        for iteration in range(ITERS):
            dead_mass = jnp.sum(rank_now * dead_ends[None, :], axis=1)
            rounded = lax.optimization_barrier((rank_now * keep_share[None, :]).astype(jnp.bfloat16))
            source = rounded.astype(jnp.float32).reshape(rank_now.shape[0], NBLK, BLK)
            padded = jnp.pad(source, ((0, 0), (1, 1), (0, 0)))
            banded = jnp.einsum("sbj,bij->sbi", padded[:, 0:NBLK], band_wide[:, 0], precision=highest)
            banded = banded + jnp.einsum("sbj,bij->sbi", padded[:, 1:NBLK + 1], band_wide[:, 1], precision=highest)
            banded = banded + jnp.einsum("sbj,bij->sbi", padded[:, 2:NBLK + 2], band_wide[:, 2], precision=highest)
            operands = jnp.take(source, sources, axis=1)
            products = jnp.einsum("stj,tij->sti", operands, off_wide, precision=highest)
            remote = jax.ops.segment_sum(jnp.moveaxis(products, 1, 0), targets, num_segments=NBLK + 1)[:NBLK]
            linked = banded + jnp.moveaxis(remote, 0, 1)
            updated = DAMP * (linked.reshape(rank_now.shape[0], NV) + dead_mass[:, None] / NV) + restart
            changes.append(jnp.sum(jnp.abs(updated - rank_now), axis=1) / NV)
            rank_now = updated
        score = jnp.sum(rank_now * seed_mask, axis=1)
        return rank_now, jnp.stack(changes), score

    group_count = 8
    ranks, changes, scores = lax.map(one_group, (rank_in.reshape(group_count, S // group_count, NV), seed_ids.reshape(group_count, S // group_count)))
    rank_out = ranks.reshape(S, NV)
    change = jnp.transpose(changes, (1, 0, 2)).reshape(ITERS, S)
    total_change = jnp.sum(change, axis=1) / S
    seed_score = scores.reshape(S)
    return rank_out, change, total_change, seed_score
```

```python
import functools

import jax
import jax.numpy as jnp
from jax import lax
from jax.experimental import pallas as pl
from jax.experimental.pallas import tpu as pltpu
from jax.sharding import PartitionSpec as P

CAP = 2
ITERS = 3
DAMP = 0.85
LANES = 128
STAT_ROWS = 8
GROUP = 16
CHUNKS = 8
VMEM_BYTES = 60 * 1024 * 1024
MESH = pl.DeviceIdType.MESH
WHOLE = pl.BlockSpec(memory_space=pltpu.VMEM)
SCALARS = pl.BlockSpec(memory_space=pltpu.SMEM)
FAR = pl.BlockSpec(memory_space=pl.ANY)


def dot_nt(a, b):
    return lax.dot_general(a, b, (((1,), (1,)), ((), ())), preferred_element_type=jnp.float32)


def greet_all(count, me):
    barrier = pltpu.get_barrier_semaphore()

    @pl.loop(1, count)
    def _(d):
        pl.semaphore_signal(
            barrier, inc=1, device_id={"dom": lax.rem(me + d, count)}, device_id_type=MESH
        )

    pl.semaphore_wait(barrier, count - 1)


def columns_to_rows(columns, seed_cols):
    lane = lax.broadcasted_iota(jnp.int32, (seed_cols, LANES), 1)
    tile = jnp.zeros((seed_cols, LANES), jnp.float32)
    for k, column in enumerate(columns):
        tile = jnp.where(lane == k, column, tile)
    square = jnp.concatenate([tile, jnp.zeros((LANES - seed_cols, LANES), jnp.float32)], axis=0)
    return square.T[:STAT_ROWS]


def row_to_column(rows, seed_cols):
    square = jnp.concatenate(
        [rows, jnp.zeros((LANES - rows.shape[0], LANES), jnp.float32)], axis=0
    )
    return square.T[:seed_cols, 0:1]


def bcast_kernel(count, stat_ref, all_ref, send_sem, recv_sem):
    me = lax.axis_index("dom")
    greet_all(count, me)

    def copy(d):
        return pltpu.make_async_remote_copy(
            src_ref=stat_ref,
            dst_ref=all_ref.at[me],
            send_sem=send_sem.at[d],
            recv_sem=recv_sem.at[d],
            device_id={"dom": lax.rem(me + d, count)},
            device_id_type=MESH,
        )

    @pl.loop(1, count)
    def _(d):
        copy(d).start()

    all_ref[me] = stat_ref[...]

    @pl.loop(1, count)
    def _(d):
        copy(d).wait()


def bcast(stat, count):
    return pl.pallas_call(
        functools.partial(bcast_kernel, count),
        out_shape=jax.ShapeDtypeStruct((count,) + stat.shape, stat.dtype),
        in_specs=[WHOLE],
        out_specs=WHOLE,
        scratch_shapes=[pltpu.SemaphoreType.DMA((count,)), pltpu.SemaphoreType.DMA((count,))],
        compiler_params=pltpu.CompilerParams(collective_id=1, has_side_effects=True),
        name="bcast_stats",
    )(stat)


def exchange_kernel(
    count, wanted_ref, src_ref, stat_ref, fetched_ref, halo_ref, all_ref,
    staging, block_send, block_recv, stat_send, stat_recv, halo_send, halo_recv,
):
    me = lax.axis_index("dom")
    blocks = src_ref.shape[0]
    greet_all(count, me)

    def block_copy(d):
        peer = lax.rem(me + d, count)
        return pltpu.make_async_remote_copy(
            src_ref=staging.at[peer],
            dst_ref=fetched_ref.at[me],
            send_sem=block_send.at[d],
            recv_sem=block_recv.at[d],
            device_id={"dom": peer},
            device_id_type=MESH,
        )

    def stat_copy(d):
        return pltpu.make_async_remote_copy(
            src_ref=stat_ref,
            dst_ref=all_ref.at[me],
            send_sem=stat_send.at[d],
            recv_sem=stat_recv.at[d],
            device_id={"dom": lax.rem(me + d, count)},
            device_id_type=MESH,
        )

    def halo_copy(side):
        step = 1 if side == 0 else count - 1
        return pltpu.make_async_remote_copy(
            src_ref=src_ref.at[blocks - 1 if side == 0 else 0],
            dst_ref=halo_ref.at[side],
            send_sem=halo_send.at[side],
            recv_sem=halo_recv.at[side],
            device_id={"dom": lax.rem(me + step, count)},
            device_id_type=MESH,
        )

    @pl.loop(1, count)
    def _(d):
        peer = lax.rem(me + d, count)
        for c in range(CAP):
            staging[peer, c] = src_ref[wanted_ref[peer * CAP + c]]
        block_copy(d).start()

    halo_copy(0).start()
    halo_copy(1).start()

    @pl.loop(1, count)
    def _(d):
        stat_copy(d).start()

    fetched_ref[me] = jnp.zeros(fetched_ref.shape[1:], fetched_ref.dtype)
    all_ref[me] = stat_ref[...]
    halo_copy(0).wait()
    halo_copy(1).wait()

    @pl.loop(1, count)
    def _(d):
        block_copy(d).wait()
        stat_copy(d).wait()


def exchange(wanted, src, stat, count):
    block = src.shape[1:]
    sems = lambda k: [pltpu.SemaphoreType.DMA((k,)), pltpu.SemaphoreType.DMA((k,))]
    return pl.pallas_call(
        functools.partial(exchange_kernel, count),
        out_shape=(
            jax.ShapeDtypeStruct((count, CAP) + block, src.dtype),
            jax.ShapeDtypeStruct((2,) + block, src.dtype),
            jax.ShapeDtypeStruct((count,) + stat.shape, stat.dtype),
        ),
        in_specs=[SCALARS, WHOLE, WHOLE],
        out_specs=(WHOLE, WHOLE, WHOLE),
        scratch_shapes=[pltpu.VMEM((count, CAP) + block, src.dtype)]
        + sems(count) + sems(count) + sems(2),
        compiler_params=pltpu.CompilerParams(
            collective_id=0, has_side_effects=True, vmem_limit_bytes=VMEM_BYTES // 2
        ),
        name="exchange_blocks",
    )(wanted, src, stat)


def init_kernel(rank_ref, dang_ref, src_ref, stat_ref):
    blocks, seed_cols, width = src_ref.shape

    def step(b, mass):
        dead = dang_ref[pl.ds(b, 1), :].astype(jnp.float32)
        rank = rank_ref[:, pl.ds(pl.multiple_of(b * width, width), width)]
        src_ref[b] = (rank * (1.0 - dead)).astype(src_ref.dtype)
        return mass + rank * dead

    mass = lax.fori_loop(0, blocks, step, jnp.zeros((seed_cols, width), jnp.float32), unroll=4)
    stat_ref[...] = columns_to_rows([jnp.sum(mass, axis=1, keepdims=True)], seed_cols)


def init(rank, dang, blocks, width):
    return pl.pallas_call(
        init_kernel,
        out_shape=(
            jax.ShapeDtypeStruct((blocks, rank.shape[0], width), jnp.bfloat16),
            jax.ShapeDtypeStruct((STAT_ROWS, LANES), jnp.float32),
        ),
        in_specs=[WHOLE, WHOLE],
        out_specs=(WHOLE, WHOLE),
        compiler_params=pltpu.CompilerParams(vmem_limit_bytes=VMEM_BYTES // 2),
        name="first_source",
    )(rank, dang)


def step_kernel(
    vertices, slot_ref, row_ref, place_ref, band_hbm, off_hbm, rank_ref, src_ref, fetched_ref,
    halo_ref, all_ref, dang_ref, seed_ref, rank_out, src_out, stat_out,
    band, off, ext, acc, band_sem, off_sem,
):
    blocks, seed_cols, width = src_ref.shape
    slots = off.shape[0]
    band_part = blocks // CHUNKS
    off_part = slots // CHUNKS
    live = place_ref[0]
    me = place_ref[1]
    last = place_ref[2]

    def band_copy(c):
        part = pl.ds(c * band_part, band_part)
        return pltpu.make_async_copy(band_hbm.at[part], band.at[part], band_sem.at[c])

    def off_copy(c):
        part = pl.ds(c * off_part, off_part)
        return pltpu.make_async_copy(off_hbm.at[part], off.at[part], off_sem.at[c])

    for c in range(CHUNKS):
        band_copy(c).start()
    for c in range(CHUNKS):
        off_copy(c).start()

    zero = jnp.zeros((seed_cols, width), ext.dtype)
    ext[0] = jnp.where(me > 0, halo_ref[0], zero)
    ext[blocks + 1] = jnp.where(me < last, halo_ref[1], zero)

    def fill(b, carry):
        ext[b + 1] = src_ref[b]
        return carry

    lax.fori_loop(0, blocks, fill, 0, unroll=8)

    @pl.loop(0, CHUNKS)
    def _(c):
        band_copy(c).wait()

        def one(i, carry):
            b = c * band_part + i
            pair = jnp.concatenate([ext[b], ext[b + 1]], axis=1)
            tiles = jnp.concatenate([band[b, 0], band[b, 1]], axis=1)
            acc[b] = dot_nt(pair, tiles) + dot_nt(ext[b + 2], band[b, 2])
            return carry

        lax.fori_loop(0, band_part, one, 0, unroll=4)

    @pl.loop(0, CHUNKS)
    def _(c):
        off_copy(c).wait()

        @pl.loop(0, off_part // GROUP)
        def _(g):
            base = c * off_part + g * GROUP

            @pl.when(base < live)
            def _():
                products = [
                    dot_nt(fetched_ref[slot_ref[base + u]], off[base + u]) for u in range(GROUP)
                ]
                for u in range(GROUP):
                    row = row_ref[base + u]
                    acc[row] = acc[row] + products[u]

    mass = row_to_column(jnp.sum(all_ref[...], axis=0), seed_cols) / vertices
    mass = jnp.broadcast_to(mass, (seed_cols, width))
    seeds = jnp.broadcast_to(seed_ref[...], (seed_cols, width)) - me * (blocks * width)
    lane = lax.broadcasted_iota(jnp.int32, (seed_cols, width), 1)
    seeds = seeds - lane

    def finish(b, carry):
        dead_mass, moved, own = carry
        here = pl.ds(pl.multiple_of(b * width, width), width)
        dead = dang_ref[pl.ds(b, 1), :].astype(jnp.float32)
        is_seed = seeds == b * width
        rank = rank_ref[:, here]
        updated = DAMP * (acc[b] + mass) + jnp.where(is_seed, 1.0 - DAMP, 0.0)
        rank_out[:, here] = updated
        src_out[b] = (updated * (1.0 - dead)).astype(src_out.dtype)
        return (
            dead_mass + updated * dead,
            moved + jnp.abs(updated - rank),
            own + jnp.where(is_seed, updated, 0.0),
        )

    nothing = jnp.zeros((seed_cols, width), jnp.float32)
    sums = lax.fori_loop(0, blocks, finish, (nothing, nothing, nothing), unroll=2)
    stat_out[...] = columns_to_rows([jnp.sum(s, axis=1, keepdims=True) for s in sums], seed_cols)


def step(vertices, slot, row, place, band, off, rank, src, fetched, halo, stats, dang, seeds):
    blocks, seed_cols, width = src.shape
    flops = 2 * seed_cols * width * width * (3 * blocks + off.shape[0])
    return pl.pallas_call(
        functools.partial(step_kernel, vertices),
        out_shape=(
            jax.ShapeDtypeStruct(rank.shape, rank.dtype),
            jax.ShapeDtypeStruct(src.shape, src.dtype),
            jax.ShapeDtypeStruct((STAT_ROWS, LANES), jnp.float32),
        ),
        in_specs=[SCALARS, SCALARS, SCALARS, FAR, FAR] + [WHOLE] * 7,
        out_specs=(WHOLE, WHOLE, WHOLE),
        scratch_shapes=[
            pltpu.VMEM(band.shape, band.dtype),
            pltpu.VMEM(off.shape, off.dtype),
            pltpu.VMEM((blocks + 2, seed_cols, width), src.dtype),
            pltpu.VMEM((blocks + 1, seed_cols, width), jnp.float32),
            pltpu.SemaphoreType.DMA((CHUNKS,)),
            pltpu.SemaphoreType.DMA((CHUNKS,)),
        ],
        compiler_params=pltpu.CompilerParams(vmem_limit_bytes=VMEM_BYTES),
        cost_estimate=pl.CostEstimate(
            flops=flops, bytes_accessed=2 * (band.size + off.size), transcendentals=0
        ),
        name="power_step",
    )(slot, row, place, band, off, rank, src, fetched, halo, stats, dang, seeds)


def plan_requests(tile_src, tile_count, blocks, count):
    source = tile_src[0]
    live = jnp.arange(source.shape[0], dtype=jnp.int32) < tile_count[0]
    holder = source // blocks
    inside = source - holder * blocks
    held = holder[None, :] == jnp.arange(count, dtype=jnp.int32)[:, None]
    read = jnp.logical_and(held, live[None, :])
    low = jnp.min(jnp.where(read, inside[None, :], blocks - 1), axis=1)
    high = jnp.max(jnp.where(read, inside[None, :], 0), axis=1)
    tile_low = jnp.sum(jnp.where(held, low[:, None], 0), axis=0)
    slot = holder * CAP + (inside != tile_low).astype(jnp.int32)
    return jnp.stack([low, high], axis=1).reshape(-1), slot, live


def on_device(rank_in, band_tiles, off_tiles, tile_src, tile_row, tile_count, seed_ids, dangling):
    blocks = band_tiles.shape[0]
    width = band_tiles.shape[2]
    seed_cols = rank_in.shape[0]
    count = lax.axis_size("dom")
    groups = lax.axis_size("seed")
    vertices = blocks * width * count
    me = lax.axis_index("dom")

    requests, slot, live = plan_requests(tile_src, tile_count, blocks, count)
    rows = jnp.where(live, tile_row[0], blocks)
    padded = jnp.pad(requests, (0, STAT_ROWS * LANES - count * CAP)).reshape(STAT_ROWS, LANES)
    asked = bcast(padded.astype(jnp.float32), count)
    asked = asked.reshape(count, STAT_ROWS * LANES)
    wanted = lax.dynamic_slice_in_dim(asked, me * CAP, CAP, axis=1)
    wanted = wanted.astype(jnp.int32).reshape(-1)

    dang = dangling.reshape(blocks, width)
    seeds = seed_ids[:, None]
    place = jnp.stack([tile_count[0], me.astype(jnp.int32), jnp.int32(count - 1)])
    rank = rank_in
    src, stat = init(rank, dang, blocks, width)
    gathered = []
    for _ in range(ITERS):
        fetched, halo, stats = exchange(wanted, src, stat, count)
        gathered.append(stats)
        fetched = fetched.reshape((count * CAP,) + src.shape[1:])
        rank, src, stat = step(
            vertices, slot, rows, place, band_tiles, off_tiles, rank, src, fetched, halo, stats,
            dang, seeds,
        )
    gathered.append(bcast(stat, count))
    moved = jnp.stack([jnp.sum(g[:, 1, :seed_cols], axis=0) for g in gathered[1:]])
    own = jnp.sum(gathered[-1][:, 2, :seed_cols], axis=0)
    change = moved / vertices
    total_change = lax.psum(jnp.sum(change, axis=1), "seed") / (seed_cols * groups)
    return (rank, change, total_change, own)


def solution(mesh):
    return jax.shard_map(
        on_device,
        mesh=mesh,
        in_specs=(
            P("seed", "dom"),
            P("dom", None, None, None),
            P("dom", None, None),
            P("dom", None),
            P("dom", None),
            P("dom"),
            P("seed"),
            P("dom"),
        ),
        out_specs=(P("seed", "dom"), P(None, "seed"), P(), P("seed")),
        check_vma=False,
    )
```

```python
import functools

import jax
import jax.numpy as jnp
from jax import lax
from jax.experimental import pallas as pl
from jax.experimental.pallas import tpu as pltpu
from jax.sharding import PartitionSpec as P

CAP = 2
ITERS = 3
DAMP = 0.85
LANES = 128
STAT_ROWS = 8
GROUP = 16
CHUNKS = 8
EARLY = 1
STEP_BYTES = 36 * 1024 * 1024
EXCHANGE_BYTES = 36 * 1024 * 1024
MESH = pl.DeviceIdType.MESH
WHOLE = pl.BlockSpec(memory_space=pltpu.VMEM)
SCALARS = pl.BlockSpec(memory_space=pltpu.SMEM)
FAR = pl.BlockSpec(memory_space=pltpu.HBM)


def dot_nt(a, b):
    return lax.dot_general(a, b, (((1,), (1,)), ((), ())), preferred_element_type=jnp.float32)


def greet_all(count, me):
    signal_all(count, me)
    pl.semaphore_wait(pltpu.get_barrier_semaphore(), count - 1)


def signal_all(count, me):
    barrier = pltpu.get_barrier_semaphore()

    @pl.loop(1, count)
    def _(d):
        pl.semaphore_signal(
            barrier, inc=1, device_id={"dom": lax.rem(me + d, count)}, device_id_type=MESH
        )


def columns_to_rows(columns, seed_cols):
    lane = lax.broadcasted_iota(jnp.int32, (seed_cols, LANES), 1)
    tile = jnp.zeros((seed_cols, LANES), jnp.float32)
    for k, column in enumerate(columns):
        tile = jnp.where(lane == k, column, tile)
    square = jnp.concatenate([tile, jnp.zeros((LANES - seed_cols, LANES), jnp.float32)], axis=0)
    return square.T[:STAT_ROWS]


def row_to_column(rows, seed_cols):
    square = jnp.concatenate(
        [rows, jnp.zeros((LANES - rows.shape[0], LANES), jnp.float32)], axis=0
    )
    return square.T[:seed_cols, 0:1]


def bcast_kernel(count, stat_ref, all_ref, send_sem, recv_sem):
    me = lax.axis_index("dom")
    greet_all(count, me)

    def copy(d):
        return pltpu.make_async_remote_copy(
            src_ref=stat_ref,
            dst_ref=all_ref.at[me],
            send_sem=send_sem.at[d],
            recv_sem=recv_sem.at[d],
            device_id={"dom": lax.rem(me + d, count)},
            device_id_type=MESH,
        )

    @pl.loop(1, count)
    def _(d):
        copy(d).start()

    all_ref[me] = stat_ref[...]

    @pl.loop(1, count)
    def _(d):
        copy(d).wait()


def bcast(stat, count):
    return pl.pallas_call(
        functools.partial(bcast_kernel, count),
        out_shape=jax.ShapeDtypeStruct((count,) + stat.shape, stat.dtype),
        in_specs=[WHOLE],
        out_specs=WHOLE,
        scratch_shapes=[pltpu.SemaphoreType.DMA((count,)), pltpu.SemaphoreType.DMA((count,))],
        compiler_params=pltpu.CompilerParams(collective_id=1, has_side_effects=True),
        name="bcast_stats",
    )(stat)


def exchange_kernel(
    count, wanted_ref, src_ref, stat_ref, band_hbm, fetched_ref, all_ref, part_ref,
    band, halo, band_sem, staging, block_send, block_recv, stat_send, stat_recv, halo_send, halo_recv,
):
    me = lax.axis_index("dom")
    blocks = src_ref.shape[0]
    band_part = blocks // CHUNKS
    signal_all(count, me)

    def band_copy(c):
        part = pl.ds(c * band_part, band_part)
        return pltpu.make_async_copy(band_hbm.at[part], band.at[part], band_sem.at[c])

    for c in range(CHUNKS):
        band_copy(c).start()

    def banded(b, left, middle, right):
        pair = jnp.concatenate([left, middle], axis=1)
        tiles = jnp.concatenate([band[b, 0], band[b, 1]], axis=1)
        part_ref[b] = dot_nt(pair, tiles) + dot_nt(right, band[b, 2])

    def band_chunk(c):
        band_copy(c).wait()

        def one(i, carry):
            b = c * band_part + i
            left = jnp.maximum(b - 1, 0)
            right = jnp.minimum(b + 1, blocks - 1)
            banded(b, src_ref[left], src_ref[b], src_ref[right])
            return carry

        lax.fori_loop(0, band_part, one, 0, unroll=4)

    def block_copy(d):
        peer = lax.rem(me + d, count)
        return pltpu.make_async_remote_copy(
            src_ref=staging.at[peer],
            dst_ref=fetched_ref.at[me],
            send_sem=block_send.at[d],
            recv_sem=block_recv.at[d],
            device_id={"dom": peer},
            device_id_type=MESH,
        )

    def stat_copy(d):
        return pltpu.make_async_remote_copy(
            src_ref=stat_ref,
            dst_ref=all_ref.at[me],
            send_sem=stat_send.at[d],
            recv_sem=stat_recv.at[d],
            device_id={"dom": lax.rem(me + d, count)},
            device_id_type=MESH,
        )

    def halo_copy(side):
        step = 1 if side == 0 else count - 1
        return pltpu.make_async_remote_copy(
            src_ref=src_ref.at[blocks - 1 if side == 0 else 0],
            dst_ref=halo.at[side],
            send_sem=halo_send.at[side],
            recv_sem=halo_recv.at[side],
            device_id={"dom": lax.rem(me + step, count)},
            device_id_type=MESH,
        )

    @pl.loop(1, count)
    def _(d):
        peer = lax.rem(me + d, count)
        for c in range(CAP):
            staging[peer, c] = src_ref[wanted_ref[peer * CAP + c]]

    fetched_ref[me] = jnp.zeros(fetched_ref.shape[1:], fetched_ref.dtype)
    all_ref[me] = stat_ref[...]
    for c in range(EARLY):
        band_chunk(c)
    pl.semaphore_wait(pltpu.get_barrier_semaphore(), count - 1)

    @pl.loop(1, count)
    def _(d):
        block_copy(d).start()

    halo_copy(0).start()
    halo_copy(1).start()

    @pl.loop(1, count)
    def _(d):
        stat_copy(d).start()

    @pl.loop(EARLY, CHUNKS)
    def _(c):
        band_chunk(c)

    halo_copy(0).wait()
    halo_copy(1).wait()
    zero = jnp.zeros(halo.shape[1:], halo.dtype)
    banded(0, jnp.where(me > 0, halo[0], zero), src_ref[0], src_ref[1])
    end = blocks - 1
    banded(end, src_ref[end - 1], src_ref[end], jnp.where(me < count - 1, halo[1], zero))

    @pl.loop(1, count)
    def _(d):
        block_copy(d).wait()
        stat_copy(d).wait()


def exchange(wanted, src, stat, band, count):
    block = src.shape[1:]
    flops = 2 * block[0] * block[1] * block[1] * 3 * src.shape[0]
    sems = lambda k: [pltpu.SemaphoreType.DMA((k,)), pltpu.SemaphoreType.DMA((k,))]
    return pl.pallas_call(
        functools.partial(exchange_kernel, count),
        out_shape=(
            jax.ShapeDtypeStruct((count, CAP) + block, src.dtype),
            jax.ShapeDtypeStruct((count,) + stat.shape, stat.dtype),
            jax.ShapeDtypeStruct(src.shape, jnp.float32),
        ),
        in_specs=[SCALARS, WHOLE, WHOLE, FAR],
        out_specs=(WHOLE, WHOLE, WHOLE),
        scratch_shapes=[
            pltpu.VMEM(band.shape, band.dtype),
            pltpu.VMEM((2,) + block, src.dtype),
            pltpu.SemaphoreType.DMA((CHUNKS,)),
            pltpu.VMEM((count, CAP) + block, src.dtype),
        ]
        + sems(count) + sems(count) + sems(2),
        compiler_params=pltpu.CompilerParams(
            collective_id=0, has_side_effects=True, vmem_limit_bytes=EXCHANGE_BYTES
        ),
        cost_estimate=pl.CostEstimate(
            flops=flops, bytes_accessed=2 * band.size, transcendentals=0
        ),
        name="exchange_blocks",
    )(wanted, src, stat, band)


def init_kernel(rank_ref, dang_ref, src_ref, stat_ref):
    blocks, seed_cols, width = src_ref.shape

    def step(b, mass):
        dead = dang_ref[pl.ds(b, 1), :].astype(jnp.float32)
        rank = rank_ref[:, pl.ds(pl.multiple_of(b * width, width), width)]
        src_ref[b] = (rank * (1.0 - dead)).astype(src_ref.dtype)
        return mass + rank * dead

    mass = lax.fori_loop(0, blocks, step, jnp.zeros((seed_cols, width), jnp.float32), unroll=4)
    stat_ref[...] = columns_to_rows([jnp.sum(mass, axis=1, keepdims=True)], seed_cols)


def init(rank, dang, blocks, width):
    return pl.pallas_call(
        init_kernel,
        out_shape=(
            jax.ShapeDtypeStruct((blocks, rank.shape[0], width), jnp.bfloat16),
            jax.ShapeDtypeStruct((STAT_ROWS, LANES), jnp.float32),
        ),
        in_specs=[WHOLE, WHOLE],
        out_specs=(WHOLE, WHOLE),
        compiler_params=pltpu.CompilerParams(vmem_limit_bytes=EXCHANGE_BYTES),
        name="first_source",
    )(rank, dang)


def step_kernel(
    vertices, slot_ref, row_ref, place_ref, off_hbm, rank_ref, part_ref, fetched_ref,
    all_ref, dang_ref, seed_ref, rank_out, src_out, stat_out, off, acc, off_sem,
):
    blocks, seed_cols, width = part_ref.shape
    slots = off.shape[0]
    off_part = slots // CHUNKS
    live = place_ref[0]
    me = place_ref[1]

    def off_copy(c):
        part = pl.ds(c * off_part, off_part)
        return pltpu.make_async_copy(off_hbm.at[part], off.at[part], off_sem.at[c])

    for c in range(CHUNKS):
        off_copy(c).start()

    def fill(b, carry):
        acc[b] = part_ref[b]
        return carry

    lax.fori_loop(0, blocks, fill, 0, unroll=4)

    @pl.loop(0, CHUNKS)
    def _(c):
        off_copy(c).wait()

        @pl.loop(0, off_part // GROUP)
        def _(g):
            base = c * off_part + g * GROUP

            @pl.when(base < live)
            def _():
                products = [
                    dot_nt(fetched_ref[slot_ref[base + u]], off[base + u]) for u in range(GROUP)
                ]
                for u in range(GROUP):
                    row = row_ref[base + u]
                    acc[row] = acc[row] + products[u]

    mass = row_to_column(jnp.sum(all_ref[...], axis=0), seed_cols) / vertices
    mass = jnp.broadcast_to(mass, (seed_cols, width))
    seeds = jnp.broadcast_to(seed_ref[...], (seed_cols, width)) - me * (blocks * width)
    lane = lax.broadcasted_iota(jnp.int32, (seed_cols, width), 1)
    seeds = seeds - lane

    def finish(b, carry):
        dead_mass, moved, own = carry
        here = pl.ds(pl.multiple_of(b * width, width), width)
        dead = dang_ref[pl.ds(b, 1), :].astype(jnp.float32)
        is_seed = seeds == b * width
        rank = rank_ref[:, here]
        updated = DAMP * (acc[b] + mass) + jnp.where(is_seed, 1.0 - DAMP, 0.0)
        rank_out[:, here] = updated
        src_out[b] = (updated * (1.0 - dead)).astype(src_out.dtype)
        return (
            dead_mass + updated * dead,
            moved + jnp.abs(updated - rank),
            own + jnp.where(is_seed, updated, 0.0),
        )

    nothing = jnp.zeros((seed_cols, width), jnp.float32)
    sums = lax.fori_loop(0, blocks, finish, (nothing, nothing, nothing), unroll=2)
    stat_out[...] = columns_to_rows([jnp.sum(s, axis=1, keepdims=True) for s in sums], seed_cols)


def step(vertices, slot, row, place, off, rank, part, fetched, stats, dang, seeds):
    blocks, seed_cols, width = part.shape
    flops = 2 * seed_cols * width * width * off.shape[0]
    return pl.pallas_call(
        functools.partial(step_kernel, vertices),
        out_shape=(
            jax.ShapeDtypeStruct(rank.shape, rank.dtype),
            jax.ShapeDtypeStruct(part.shape, fetched.dtype),
            jax.ShapeDtypeStruct((STAT_ROWS, LANES), jnp.float32),
        ),
        in_specs=[SCALARS, SCALARS, SCALARS, FAR] + [WHOLE] * 6,
        out_specs=(WHOLE, WHOLE, WHOLE),
        scratch_shapes=[
            pltpu.VMEM(off.shape, off.dtype),
            pltpu.VMEM((blocks + 1, seed_cols, width), jnp.float32),
            pltpu.SemaphoreType.DMA((CHUNKS,)),
        ],
        compiler_params=pltpu.CompilerParams(vmem_limit_bytes=STEP_BYTES),
        cost_estimate=pl.CostEstimate(
            flops=flops, bytes_accessed=2 * off.size, transcendentals=0
        ),
        name="power_step",
    )(slot, row, place, off, rank, part, fetched, stats, dang, seeds)


def plan_requests(tile_src, tile_count, blocks, count):
    source = tile_src[0]
    live = jnp.arange(source.shape[0], dtype=jnp.int32) < tile_count[0]
    holder = source // blocks
    inside = source - holder * blocks
    held = holder[None, :] == jnp.arange(count, dtype=jnp.int32)[:, None]
    read = jnp.logical_and(held, live[None, :])
    low = jnp.min(jnp.where(read, inside[None, :], blocks - 1), axis=1)
    high = jnp.max(jnp.where(read, inside[None, :], 0), axis=1)
    tile_low = jnp.sum(jnp.where(held, low[:, None], 0), axis=0)
    slot = holder * CAP + (inside != tile_low).astype(jnp.int32)
    return jnp.stack([low, high], axis=1).reshape(-1), slot, live


def on_device(rank_in, band_tiles, off_tiles, tile_src, tile_row, tile_count, seed_ids, dangling):
    blocks = band_tiles.shape[0]
    width = band_tiles.shape[2]
    seed_cols = rank_in.shape[0]
    count = lax.axis_size("dom")
    groups = lax.axis_size("seed")
    vertices = blocks * width * count
    me = lax.axis_index("dom")

    requests, slot, live = plan_requests(tile_src, tile_count, blocks, count)
    rows = jnp.where(live, tile_row[0], blocks)
    padded = jnp.pad(requests, (0, STAT_ROWS * LANES - count * CAP)).reshape(STAT_ROWS, LANES)
    asked = bcast(padded.astype(jnp.float32), count)
    asked = asked.reshape(count, STAT_ROWS * LANES)
    wanted = lax.dynamic_slice_in_dim(asked, me * CAP, CAP, axis=1)
    wanted = wanted.astype(jnp.int32).reshape(-1)

    dang = dangling.reshape(blocks, width)
    seeds = seed_ids[:, None]
    place = jnp.stack([tile_count[0], me.astype(jnp.int32)])
    rank = rank_in
    src, stat = init(rank, dang, blocks, width)
    gathered = []
    for _ in range(ITERS):
        fetched, stats, part = exchange(wanted, src, stat, band_tiles, count)
        gathered.append(stats)
        fetched = fetched.reshape((count * CAP,) + src.shape[1:])
        rank, src, stat = step(
            vertices, slot, rows, place, off_tiles, rank, part, fetched, stats, dang, seeds
        )
    gathered.append(bcast(stat, count))
    moved = jnp.stack([jnp.sum(g[:, 1, :seed_cols], axis=0) for g in gathered[1:]])
    own = jnp.sum(gathered[-1][:, 2, :seed_cols], axis=0)
    change = moved / vertices
    total_change = lax.psum(jnp.sum(change, axis=1), "seed") / (seed_cols * groups)
    return (rank, change, total_change, own)


def solution(mesh):
    return jax.shard_map(
        on_device,
        mesh=mesh,
        in_specs=(
            P("seed", "dom"),
            P("dom", None, None, None),
            P("dom", None, None),
            P("dom", None),
            P("dom", None),
            P("dom"),
            P("seed"),
            P("dom"),
        ),
        out_specs=(P("seed", "dom"), P(None, "seed"), P(), P("seed")),
        check_vma=False,
    )
```

```python
import functools

import jax
import jax.numpy as jnp
from jax import lax
from jax.experimental import pallas as pl
from jax.experimental.pallas import tpu as pltpu
from jax.sharding import PartitionSpec as P

CAP = 2
ITERS = 3
DAMP = 0.85
LANES = 128
STAT_ROWS = 8
GROUP = 32
CHUNKS = 8
EARLY = 1
STEP_BYTES = 36 * 1024 * 1024
FIRST_BYTES = 48 * 1024 * 1024
EXCHANGE_BYTES = 36 * 1024 * 1024
MESH = pl.DeviceIdType.MESH
WHOLE = pl.BlockSpec(memory_space=pltpu.VMEM)
SCALARS = pl.BlockSpec(memory_space=pltpu.SMEM)
FAR = pl.BlockSpec(memory_space=pltpu.HBM)


def dot_nt(a, b):
    return lax.dot_general(a, b, (((1,), (1,)), ((), ())), preferred_element_type=jnp.float32)


def signal_all(count, me):
    barrier = pltpu.get_barrier_semaphore()

    @pl.loop(1, count)
    def _(d):
        pl.semaphore_signal(
            barrier, inc=1, device_id={"dom": lax.rem(me + d, count)}, device_id_type=MESH
        )


def columns_to_rows(columns, seed_cols):
    lane = lax.broadcasted_iota(jnp.int32, (seed_cols, LANES), 1)
    tile = jnp.zeros((seed_cols, LANES), jnp.float32)
    for k, column in columns.items():
        tile = jnp.where(lane == k, column, tile)
    square = jnp.concatenate([tile, jnp.zeros((LANES - seed_cols, LANES), jnp.float32)], axis=0)
    return square.T[:STAT_ROWS]


def row_to_column(rows, seed_cols):
    square = jnp.concatenate(
        [rows, jnp.zeros((LANES - rows.shape[0], LANES), jnp.float32)], axis=0
    )
    return square.T[:seed_cols, 0:1]


def first_kernel(
    count, request_ref, dang_ref, rank_hbm, asked_ref, src_ref, mass_ref,
    rank, rank_sem, send_sem, recv_sem,
):
    me = lax.axis_index("dom")
    blocks, seed_cols, width = src_ref.shape
    part = blocks // CHUNKS
    signal_all(count, me)

    def rank_copy(c):
        here = pl.ds(c * part * width, part * width)
        return pltpu.make_async_copy(rank_hbm.at[:, here], rank.at[:, here], rank_sem.at[c])

    for c in range(CHUNKS):
        rank_copy(c).start()
    pl.semaphore_wait(pltpu.get_barrier_semaphore(), count - 1)

    def copy(d):
        return pltpu.make_async_remote_copy(
            src_ref=request_ref,
            dst_ref=asked_ref.at[me],
            send_sem=send_sem.at[d],
            recv_sem=recv_sem.at[d],
            device_id={"dom": lax.rem(me + d, count)},
            device_id_type=MESH,
        )

    @pl.loop(1, count)
    def _(d):
        copy(d).start()

    asked_ref[me] = request_ref[...]
    mass_ref[...] = jnp.zeros(mass_ref.shape, mass_ref.dtype)

    @pl.loop(0, CHUNKS)
    def _(c):
        rank_copy(c).wait()

        def one(i, mass):
            b = c * part + i
            dead = dang_ref[pl.ds(b, 1), :].astype(jnp.float32)
            now = rank[:, pl.ds(pl.multiple_of(b * width, width), width)]
            src_ref[b] = (now * (1.0 - dead)).astype(src_ref.dtype)
            return mass + now * dead

        mass_ref[...] = lax.fori_loop(0, part, one, mass_ref[...], unroll=4)

    @pl.loop(1, count)
    def _(d):
        copy(d).wait()


def first(request, dang, rank, blocks, width, count):
    seed_cols = rank.shape[0]
    return pl.pallas_call(
        functools.partial(first_kernel, count),
        out_shape=(
            jax.ShapeDtypeStruct((count,) + request.shape, request.dtype),
            jax.ShapeDtypeStruct((blocks, seed_cols, width), jnp.bfloat16),
            jax.ShapeDtypeStruct((seed_cols, width), jnp.float32),
        ),
        in_specs=[WHOLE, WHOLE, FAR],
        out_specs=(WHOLE, WHOLE, WHOLE),
        scratch_shapes=[
            pltpu.VMEM(rank.shape, rank.dtype),
            pltpu.SemaphoreType.DMA((CHUNKS,)),
            pltpu.SemaphoreType.DMA((count,)),
            pltpu.SemaphoreType.DMA((count,)),
        ],
        compiler_params=pltpu.CompilerParams(
            collective_id=1, has_side_effects=True, vmem_limit_bytes=FIRST_BYTES
        ),
        name="first_source",
    )(request, dang, rank)


def last_kernel(count, groups, stat_ref, mine_ref, whole_ref, tiles, send_sem, recv_sem):
    total = count * groups
    group = lax.axis_index("seed")
    me = group * count + lax.axis_index("dom")
    barrier = pltpu.get_barrier_semaphore()

    def device(k):
        peer = lax.rem(me + k, total)
        return {"dom": lax.rem(peer, count), "seed": peer // count}

    @pl.loop(1, total)
    def _(k):
        pl.semaphore_signal(barrier, inc=1, device_id=device(k), device_id_type=MESH)

    pl.semaphore_wait(barrier, total - 1)

    def copy(k):
        return pltpu.make_async_remote_copy(
            src_ref=stat_ref,
            dst_ref=tiles.at[me],
            send_sem=send_sem.at[k],
            recv_sem=recv_sem.at[k],
            device_id=device(k),
            device_id_type=MESH,
        )

    @pl.loop(1, total)
    def _(k):
        copy(k).start()

    tiles[me] = stat_ref[...]

    @pl.loop(1, total)
    def _(k):
        copy(k).wait()

    def added(first, end):
        zero = jnp.zeros(stat_ref.shape, stat_ref.dtype)
        return lax.fori_loop(0, end, lambda i, t: t + tiles[first + i], zero)

    mine_ref[...] = added(group * count, count)
    whole_ref[...] = added(0, total)


def last(stat, count, groups):
    total = count * groups
    tile = jax.ShapeDtypeStruct(stat.shape, stat.dtype)
    return pl.pallas_call(
        functools.partial(last_kernel, count, groups),
        out_shape=(tile, tile),
        in_specs=[WHOLE],
        out_specs=(WHOLE, WHOLE),
        scratch_shapes=[
            pltpu.VMEM((total,) + stat.shape, stat.dtype),
            pltpu.SemaphoreType.DMA((total,)),
            pltpu.SemaphoreType.DMA((total,)),
        ],
        compiler_params=pltpu.CompilerParams(collective_id=2, has_side_effects=True),
        name="last_sums",
    )(stat)


def exchange_kernel(
    count, wanted_ref, src_ref, stat_ref, band_hbm, fetched_ref, all_ref, part_ref,
    band, halo, band_sem, staging, block_send, block_recv, stat_send, stat_recv, halo_send, halo_recv,
):
    me = lax.axis_index("dom")
    blocks = src_ref.shape[0]
    band_part = blocks // CHUNKS
    signal_all(count, me)

    def band_copy(c):
        part = pl.ds(c * band_part, band_part)
        return pltpu.make_async_copy(band_hbm.at[part], band.at[part], band_sem.at[c])

    for c in range(CHUNKS):
        band_copy(c).start()

    def banded(b, left, middle, right):
        pair = jnp.concatenate([left, middle], axis=1)
        tiles = jnp.concatenate([band[b, 0], band[b, 1]], axis=1)
        part_ref[b] = dot_nt(pair, tiles) + dot_nt(right, band[b, 2])

    def band_chunk(c):
        band_copy(c).wait()

        def one(i, carry):
            b = c * band_part + i
            left = jnp.maximum(b - 1, 0)
            right = jnp.minimum(b + 1, blocks - 1)
            banded(b, src_ref[left], src_ref[b], src_ref[right])
            return carry

        lax.fori_loop(0, band_part, one, 0, unroll=4)

    def block_copy(d):
        peer = lax.rem(me + d, count)
        return pltpu.make_async_remote_copy(
            src_ref=staging.at[peer],
            dst_ref=fetched_ref.at[me],
            send_sem=block_send.at[d],
            recv_sem=block_recv.at[d],
            device_id={"dom": peer},
            device_id_type=MESH,
        )

    def stat_copy(d):
        return pltpu.make_async_remote_copy(
            src_ref=stat_ref,
            dst_ref=all_ref.at[me],
            send_sem=stat_send.at[d],
            recv_sem=stat_recv.at[d],
            device_id={"dom": lax.rem(me + d, count)},
            device_id_type=MESH,
        )

    def halo_copy(side):
        step = 1 if side == 0 else count - 1
        return pltpu.make_async_remote_copy(
            src_ref=src_ref.at[blocks - 1 if side == 0 else 0],
            dst_ref=halo.at[side],
            send_sem=halo_send.at[side],
            recv_sem=halo_recv.at[side],
            device_id={"dom": lax.rem(me + step, count)},
            device_id_type=MESH,
        )

    @pl.loop(1, count)
    def _(d):
        peer = lax.rem(me + d, count)
        for c in range(CAP):
            staging[peer, c] = src_ref[wanted_ref[peer * CAP + c]]

    fetched_ref[me] = jnp.zeros(fetched_ref.shape[1:], fetched_ref.dtype)
    all_ref[me] = stat_ref[...]
    for c in range(EARLY):
        band_chunk(c)
    pl.semaphore_wait(pltpu.get_barrier_semaphore(), count - 1)

    @pl.loop(1, count)
    def _(d):
        block_copy(d).start()

    halo_copy(0).start()
    halo_copy(1).start()

    @pl.loop(1, count)
    def _(d):
        stat_copy(d).start()

    @pl.loop(EARLY, CHUNKS)
    def _(c):
        band_chunk(c)

    halo_copy(0).wait()
    halo_copy(1).wait()
    zero = jnp.zeros(halo.shape[1:], halo.dtype)
    banded(0, jnp.where(me > 0, halo[0], zero), src_ref[0], src_ref[1])
    end = blocks - 1
    banded(end, src_ref[end - 1], src_ref[end], jnp.where(me < count - 1, halo[1], zero))

    @pl.loop(1, count)
    def _(d):
        block_copy(d).wait()
        stat_copy(d).wait()


def exchange(wanted, src, stat, band, count):
    block = src.shape[1:]
    flops = 2 * block[0] * block[1] * block[1] * 3 * src.shape[0]
    sems = lambda k: [pltpu.SemaphoreType.DMA((k,)), pltpu.SemaphoreType.DMA((k,))]
    return pl.pallas_call(
        functools.partial(exchange_kernel, count),
        out_shape=(
            jax.ShapeDtypeStruct((count, CAP) + block, src.dtype),
            jax.ShapeDtypeStruct((count,) + stat.shape, stat.dtype),
            jax.ShapeDtypeStruct(src.shape, jnp.float32),
        ),
        in_specs=[SCALARS, WHOLE, WHOLE, FAR],
        out_specs=(WHOLE, WHOLE, WHOLE),
        scratch_shapes=[
            pltpu.VMEM(band.shape, band.dtype),
            pltpu.VMEM((2,) + block, src.dtype),
            pltpu.SemaphoreType.DMA((CHUNKS,)),
            pltpu.VMEM((count, CAP) + block, src.dtype),
        ]
        + sems(count) + sems(count) + sems(2),
        compiler_params=pltpu.CompilerParams(
            collective_id=0, has_side_effects=True, vmem_limit_bytes=EXCHANGE_BYTES
        ),
        cost_estimate=pl.CostEstimate(
            flops=flops, bytes_accessed=2 * band.size, transcendentals=0
        ),
        name="exchange_blocks",
    )(wanted, src, stat, band)


def step_kernel(
    vertices, iteration, final, slot_ref, row_ref, place_ref, off_hbm, rank_ref, part_ref, fetched_ref,
    all_ref, dang_ref, seed_ref, stat_ref, rank_out, *rest,
):
    if final:
        stat_out, off, acc, off_sem, rank_new, rank_sem = rest
    else:
        src_out, stat_out, off, acc, off_sem = rest
        rank_new = rank_out
    blocks, seed_cols, width = part_ref.shape
    slots = off.shape[0]
    off_part = slots // CHUNKS
    live = place_ref[0]
    me = place_ref[1]

    def off_copy(c):
        part = pl.ds(c * off_part, off_part)
        return pltpu.make_async_copy(off_hbm.at[part], off.at[part], off_sem.at[c])

    for c in range(CHUNKS):
        off_copy(c).start()

    def fill(b, carry):
        acc[b] = part_ref[b]
        return carry

    lax.fori_loop(0, blocks, fill, 0, unroll=4)

    @pl.loop(0, CHUNKS)
    def _(c):
        off_copy(c).wait()

        @pl.loop(0, off_part // GROUP)
        def _(g):
            base = c * off_part + g * GROUP

            @pl.when(base < live)
            def _():
                products = [
                    dot_nt(fetched_ref[slot_ref[base + u]], off[base + u]) for u in range(GROUP)
                ]
                for u in range(GROUP):
                    row = row_ref[base + u]
                    acc[row] = acc[row] + products[u]

    mass = row_to_column(jnp.sum(all_ref[...], axis=0), seed_cols) / vertices
    mass = jnp.broadcast_to(mass, (seed_cols, width))
    seeds = jnp.broadcast_to(seed_ref[...], (seed_cols, width)) - me * (blocks * width)
    lane = lax.broadcasted_iota(jnp.int32, (seed_cols, width), 1)
    seeds = seeds - lane

    def finish(b, carry):
        dead_mass, moved, own = carry
        here = pl.ds(pl.multiple_of(b * width, width), width)
        dead = dang_ref[pl.ds(b, 1), :].astype(jnp.float32)
        is_seed = seeds == b * width
        rank = rank_ref[:, here]
        updated = DAMP * (acc[b] + mass) + jnp.where(is_seed, 1.0 - DAMP, 0.0)
        rank_new[:, here] = updated
        if not final:
            src_out[b] = (updated * (1.0 - dead)).astype(src_out.dtype)
        return (
            dead_mass + updated * dead,
            moved + jnp.abs(updated - rank),
            own + jnp.where(is_seed, updated, 0.0),
        )

    nothing = jnp.zeros((seed_cols, width), jnp.float32)
    part = blocks // CHUNKS

    def rank_copy(c):
        here = pl.ds(c * part * width, part * width)
        return pltpu.make_async_copy(rank_new.at[:, here], rank_out.at[:, here], rank_sem.at[c])

    sums = (nothing, nothing, nothing)
    for c in range(CHUNKS):
        sums = lax.fori_loop(c * part, (c + 1) * part, finish, sums, unroll=4)
        if final:
            rank_copy(c).start()
    mass, moved, own = [jnp.sum(s, axis=1, keepdims=True) for s in sums]
    rows = columns_to_rows({0: mass, 1: own, 2 + iteration: moved}, seed_cols)
    kind = lax.broadcasted_iota(jnp.int32, rows.shape, 0)
    stat_out[...] = rows + jnp.where(kind >= 2, stat_ref[...], 0.0)
    if final:
        for c in range(CHUNKS):
            rank_copy(c).wait()


def step(vertices, iteration, slot, row, place, off, rank, part, fetched, stats, dang, seeds, stat):
    final = iteration == ITERS - 1
    blocks, seed_cols, width = part.shape
    flops = 2 * seed_cols * width * width * off.shape[0]
    rank_type = jax.ShapeDtypeStruct(rank.shape, rank.dtype)
    src_type = jax.ShapeDtypeStruct(part.shape, fetched.dtype)
    stat_type = jax.ShapeDtypeStruct(stat.shape, stat.dtype)
    return pl.pallas_call(
        functools.partial(step_kernel, vertices, iteration, final),
        out_shape=(rank_type, stat_type) if final else (rank_type, src_type, stat_type),
        in_specs=[SCALARS, SCALARS, SCALARS, FAR] + [WHOLE] * 7,
        out_specs=(FAR, WHOLE) if final else (WHOLE, WHOLE, WHOLE),
        scratch_shapes=[
            pltpu.VMEM(off.shape, off.dtype),
            pltpu.VMEM((blocks + 1, seed_cols, width), jnp.float32),
            pltpu.SemaphoreType.DMA((CHUNKS,)),
        ]
        + ([pltpu.VMEM(rank.shape, rank.dtype), pltpu.SemaphoreType.DMA((CHUNKS,))] if final else []),
        compiler_params=pltpu.CompilerParams(vmem_limit_bytes=STEP_BYTES),
        cost_estimate=pl.CostEstimate(
            flops=flops, bytes_accessed=2 * off.size, transcendentals=0
        ),
        name="power_step",
    )(slot, row, place, off, rank, part, fetched, stats, dang, seeds, stat)


def plan_requests(tile_src, tile_count, blocks, count):
    source = tile_src[0]
    live = jnp.arange(source.shape[0], dtype=jnp.int32) < tile_count[0]
    holder = source // blocks
    inside = source - holder * blocks
    held = holder[None, :] == jnp.arange(count, dtype=jnp.int32)[:, None]
    read = jnp.logical_and(held, live[None, :])
    low = jnp.min(jnp.where(read, inside[None, :], blocks - 1), axis=1)
    high = jnp.max(jnp.where(read, inside[None, :], 0), axis=1)
    tile_low = jnp.sum(jnp.where(held, low[:, None], 0), axis=0)
    slot = holder * CAP + (inside != tile_low).astype(jnp.int32)
    return jnp.stack([low, high], axis=1).reshape(-1), slot, live


def on_device(rank_in, band_tiles, off_tiles, tile_src, tile_row, tile_count, seed_ids, dangling):
    blocks = band_tiles.shape[0]
    width = band_tiles.shape[2]
    seed_cols = rank_in.shape[0]
    count = lax.axis_size("dom")
    groups = lax.axis_size("seed")
    vertices = blocks * width * count
    me = lax.axis_index("dom")

    requests, slot, live = plan_requests(tile_src, tile_count, blocks, count)
    rows = jnp.where(live, tile_row[0], blocks)
    padded = jnp.pad(requests, (0, STAT_ROWS * LANES - count * CAP)).reshape(STAT_ROWS, LANES)
    dang = dangling.reshape(blocks, width)
    asked, src, mass = first(padded.astype(jnp.float32), dang, rank_in, blocks, width, count)
    asked = asked.reshape(count, STAT_ROWS * LANES)
    wanted = lax.dynamic_slice_in_dim(asked, me * CAP, CAP, axis=1)
    wanted = wanted.astype(jnp.int32).reshape(-1)
    stat = jnp.pad(
        jnp.sum(mass, axis=1)[None, :], ((0, STAT_ROWS - 1), (0, LANES - seed_cols))
    )

    seeds = seed_ids[:, None]
    place = jnp.stack([tile_count[0], me.astype(jnp.int32)])
    rank = rank_in
    for iteration in range(ITERS):
        fetched, stats, part = exchange(wanted, src, stat, band_tiles, count)
        fetched = fetched.reshape((count * CAP,) + src.shape[1:])
        rank, *src, stat = step(
            vertices, iteration, slot, rows, place, off_tiles, rank, part, fetched, stats, dang,
            seeds, stat,
        )
        src = src[0] if src else None
    mine, whole = last(stat, count, groups)
    change = mine[2 : 2 + ITERS, :seed_cols] / vertices
    total_change = jnp.sum(whole[2 : 2 + ITERS], axis=1) / vertices / (seed_cols * groups)
    return (rank, change, total_change, mine[1, :seed_cols])


def solution(mesh):
    return jax.shard_map(
        on_device,
        mesh=mesh,
        in_specs=(
            P("seed", "dom"),
            P("dom", None, None, None),
            P("dom", None, None),
            P("dom", None),
            P("dom", None),
            P("dom"),
            P("seed"),
            P("dom"),
        ),
        out_specs=(P("seed", "dom"), P(None, "seed"), P(), P("seed")),
        check_vma=False,
    )
```

```python
import functools

import jax
import jax.numpy as jnp
from jax import lax
from jax.experimental import pallas as pl
from jax.experimental.pallas import tpu as pltpu
from jax.sharding import PartitionSpec as P

CAP = 2
ITERS = 3
DAMP = 0.85
LANES = 128
STAT_ROWS = 8
GROUP = 64
CHUNKS = 8
STEP_BYTES = 36 * 1024 * 1024
FIRST_BYTES = 48 * 1024 * 1024
EXCHANGE_BYTES = 36 * 1024 * 1024
MESH = pl.DeviceIdType.MESH
WHOLE = pl.BlockSpec(memory_space=pltpu.VMEM)
SCALARS = pl.BlockSpec(memory_space=pltpu.SMEM)
FAR = pl.BlockSpec(memory_space=pltpu.HBM)


def dot_nt(a, b):
    return lax.dot_general(a, b, (((1,), (1,)), ((), ())), preferred_element_type=jnp.float32)


def signal_all(count, me):
    barrier = pltpu.get_barrier_semaphore()

    @pl.loop(1, count)
    def _(d):
        pl.semaphore_signal(
            barrier, inc=1, device_id={"dom": lax.rem(me + d, count)}, device_id_type=MESH
        )


def columns_to_rows(columns, seed_cols):
    lane = lax.broadcasted_iota(jnp.int32, (seed_cols, LANES), 1)
    tile = jnp.zeros((seed_cols, LANES), jnp.float32)
    for k, column in columns.items():
        tile = jnp.where(lane == k, column, tile)
    square = jnp.concatenate([tile, jnp.zeros((LANES - seed_cols, LANES), jnp.float32)], axis=0)
    return square.T[:STAT_ROWS]


def row_to_column(rows, seed_cols):
    square = jnp.concatenate(
        [rows, jnp.zeros((LANES - rows.shape[0], LANES), jnp.float32)], axis=0
    )
    return square.T[:seed_cols, 0:1]


def first_kernel(
    count, request_ref, dang_ref, rank_hbm, asked_ref, src_ref, mass_ref,
    rank, rank_sem, send_sem, recv_sem,
):
    me = lax.axis_index("dom")
    blocks, seed_cols, width = src_ref.shape
    part = blocks // CHUNKS
    signal_all(count, me)

    def rank_copy(c):
        here = pl.ds(c * part * width, part * width)
        return pltpu.make_async_copy(rank_hbm.at[:, here], rank.at[:, here], rank_sem.at[c])

    for c in range(CHUNKS):
        rank_copy(c).start()
    pl.semaphore_wait(pltpu.get_barrier_semaphore(), count - 1)

    def copy(d):
        return pltpu.make_async_remote_copy(
            src_ref=request_ref,
            dst_ref=asked_ref.at[me],
            send_sem=send_sem.at[d],
            recv_sem=recv_sem.at[d],
            device_id={"dom": lax.rem(me + d, count)},
            device_id_type=MESH,
        )

    @pl.loop(1, count)
    def _(d):
        copy(d).start()

    asked_ref[me] = request_ref[...]
    mass_ref[...] = jnp.zeros(mass_ref.shape, mass_ref.dtype)

    @pl.loop(0, CHUNKS)
    def _(c):
        rank_copy(c).wait()

        def one(i, mass):
            b = c * part + i
            dead = dang_ref[pl.ds(b, 1), :].astype(jnp.float32)
            now = rank[:, pl.ds(pl.multiple_of(b * width, width), width)]
            src_ref[b] = (now * (1.0 - dead)).astype(src_ref.dtype)
            return mass + now * dead

        mass_ref[...] = lax.fori_loop(0, part, one, mass_ref[...], unroll=4)

    @pl.loop(1, count)
    def _(d):
        copy(d).wait()


def first(request, dang, rank, blocks, width, count):
    seed_cols = rank.shape[0]
    return pl.pallas_call(
        functools.partial(first_kernel, count),
        out_shape=(
            jax.ShapeDtypeStruct((count,) + request.shape, request.dtype),
            jax.ShapeDtypeStruct((blocks, seed_cols, width), jnp.bfloat16),
            jax.ShapeDtypeStruct((seed_cols, width), jnp.float32),
        ),
        in_specs=[WHOLE, WHOLE, FAR],
        out_specs=(WHOLE, WHOLE, WHOLE),
        scratch_shapes=[
            pltpu.VMEM(rank.shape, rank.dtype),
            pltpu.SemaphoreType.DMA((CHUNKS,)),
            pltpu.SemaphoreType.DMA((count,)),
            pltpu.SemaphoreType.DMA((count,)),
        ],
        compiler_params=pltpu.CompilerParams(
            collective_id=1, has_side_effects=True, vmem_limit_bytes=FIRST_BYTES
        ),
        name="first_source",
    )(request, dang, rank)


def last_kernel(count, groups, stat_ref, mine_ref, whole_ref, tiles, send_sem, recv_sem):
    total = count * groups
    group = lax.axis_index("seed")
    me = group * count + lax.axis_index("dom")
    barrier = pltpu.get_barrier_semaphore()

    def device(k):
        peer = lax.rem(me + k, total)
        return {"dom": lax.rem(peer, count), "seed": peer // count}

    @pl.loop(1, total)
    def _(k):
        pl.semaphore_signal(barrier, inc=1, device_id=device(k), device_id_type=MESH)

    pl.semaphore_wait(barrier, total - 1)

    def copy(k):
        return pltpu.make_async_remote_copy(
            src_ref=stat_ref,
            dst_ref=tiles.at[me],
            send_sem=send_sem.at[k],
            recv_sem=recv_sem.at[k],
            device_id=device(k),
            device_id_type=MESH,
        )

    @pl.loop(1, total)
    def _(k):
        copy(k).start()

    tiles[me] = stat_ref[...]

    @pl.loop(1, total)
    def _(k):
        copy(k).wait()

    def added(first, end):
        zero = jnp.zeros(stat_ref.shape, stat_ref.dtype)
        return lax.fori_loop(0, end, lambda i, t: t + tiles[first + i], zero)

    mine_ref[...] = added(group * count, count)
    whole_ref[...] = added(0, total)


def last(stat, count, groups):
    total = count * groups
    tile = jax.ShapeDtypeStruct(stat.shape, stat.dtype)
    return pl.pallas_call(
        functools.partial(last_kernel, count, groups),
        out_shape=(tile, tile),
        in_specs=[WHOLE],
        out_specs=(WHOLE, WHOLE),
        scratch_shapes=[
            pltpu.VMEM((total,) + stat.shape, stat.dtype),
            pltpu.SemaphoreType.DMA((total,)),
            pltpu.SemaphoreType.DMA((total,)),
        ],
        compiler_params=pltpu.CompilerParams(collective_id=2, has_side_effects=True),
        name="last_sums",
    )(stat)


def exchange_kernel(
    count, wanted_ref, src_ref, stat_ref, band_hbm, fetched_ref, all_ref, part_ref,
    band, halo, band_sem, staging, block_send, block_recv, stat_send, stat_recv, halo_send, halo_recv,
):
    me = lax.axis_index("dom")
    blocks = src_ref.shape[0]
    band_part = blocks // CHUNKS
    signal_all(count, me)

    def band_copy(c):
        part = pl.ds(c * band_part, band_part)
        return pltpu.make_async_copy(band_hbm.at[part], band.at[part], band_sem.at[c])

    for c in range(CHUNKS):
        band_copy(c).start()

    def banded(b, left, middle, right):
        pair = jnp.concatenate([left, middle], axis=1)
        tiles = jnp.concatenate([band[b, 0], band[b, 1]], axis=1)
        part_ref[b] = dot_nt(pair, tiles) + dot_nt(right, band[b, 2])

    def band_chunk(c):
        band_copy(c).wait()

        def one(i, carry):
            b = c * band_part + i
            left = jnp.maximum(b - 1, 0)
            right = jnp.minimum(b + 1, blocks - 1)
            banded(b, src_ref[left], src_ref[b], src_ref[right])
            return carry

        lax.fori_loop(0, band_part, one, 0, unroll=4)

    def block_copy(d):
        peer = lax.rem(me + d, count)
        return pltpu.make_async_remote_copy(
            src_ref=staging.at[peer],
            dst_ref=fetched_ref.at[me],
            send_sem=block_send.at[d],
            recv_sem=block_recv.at[d],
            device_id={"dom": peer},
            device_id_type=MESH,
        )

    def stat_copy(d):
        return pltpu.make_async_remote_copy(
            src_ref=stat_ref,
            dst_ref=all_ref.at[me],
            send_sem=stat_send.at[d],
            recv_sem=stat_recv.at[d],
            device_id={"dom": lax.rem(me + d, count)},
            device_id_type=MESH,
        )

    def halo_copy(side):
        step = 1 if side == 0 else count - 1
        return pltpu.make_async_remote_copy(
            src_ref=src_ref.at[blocks - 1 if side == 0 else 0],
            dst_ref=halo.at[side],
            send_sem=halo_send.at[side],
            recv_sem=halo_recv.at[side],
            device_id={"dom": lax.rem(me + step, count)},
            device_id_type=MESH,
        )

    @pl.loop(1, count)
    def _(d):
        peer = lax.rem(me + d, count)
        for c in range(CAP):
            staging[peer, c] = src_ref[wanted_ref[peer * CAP + c]]

    fetched_ref[me] = jnp.zeros(fetched_ref.shape[1:], fetched_ref.dtype)
    all_ref[me] = stat_ref[...]
    pl.semaphore_wait(pltpu.get_barrier_semaphore(), count - 1)

    @pl.loop(1, count)
    def _(d):
        block_copy(d).start()

    halo_copy(0).start()
    halo_copy(1).start()

    @pl.loop(1, count)
    def _(d):
        stat_copy(d).start()

    @pl.loop(0, CHUNKS)
    def _(c):
        band_chunk(c)

    halo_copy(0).wait()
    halo_copy(1).wait()
    zero = jnp.zeros(halo.shape[1:], halo.dtype)
    banded(0, jnp.where(me > 0, halo[0], zero), src_ref[0], src_ref[1])
    end = blocks - 1
    banded(end, src_ref[end - 1], src_ref[end], jnp.where(me < count - 1, halo[1], zero))

    @pl.loop(1, count)
    def _(d):
        block_copy(d).wait()
        stat_copy(d).wait()


def exchange(wanted, src, stat, band, count):
    block = src.shape[1:]
    flops = 2 * block[0] * block[1] * block[1] * 3 * src.shape[0]
    sems = lambda k: [pltpu.SemaphoreType.DMA((k,)), pltpu.SemaphoreType.DMA((k,))]
    return pl.pallas_call(
        functools.partial(exchange_kernel, count),
        out_shape=(
            jax.ShapeDtypeStruct((count, CAP) + block, src.dtype),
            jax.ShapeDtypeStruct((count,) + stat.shape, stat.dtype),
            jax.ShapeDtypeStruct(src.shape, jnp.float32),
        ),
        in_specs=[SCALARS, WHOLE, WHOLE, FAR],
        out_specs=(WHOLE, WHOLE, WHOLE),
        scratch_shapes=[
            pltpu.VMEM(band.shape, band.dtype),
            pltpu.VMEM((2,) + block, src.dtype),
            pltpu.SemaphoreType.DMA((CHUNKS,)),
            pltpu.VMEM((count, CAP) + block, src.dtype),
        ]
        + sems(count) + sems(count) + sems(2),
        compiler_params=pltpu.CompilerParams(
            collective_id=0, has_side_effects=True, vmem_limit_bytes=EXCHANGE_BYTES
        ),
        cost_estimate=pl.CostEstimate(
            flops=flops, bytes_accessed=2 * band.size, transcendentals=0
        ),
        name="exchange_blocks",
    )(wanted, src, stat, band)


def step_kernel(
    vertices, iteration, final, slot_ref, row_ref, place_ref, off_hbm, rank_ref, part_ref, fetched_ref,
    all_ref, dang_ref, seed_ref, stat_ref, rank_out, *rest,
):
    if final:
        stat_out, off, acc, off_sem, rank_new, rank_sem = rest
    else:
        src_out, stat_out, off, acc, off_sem = rest
        rank_new = rank_out
    blocks, seed_cols, width = part_ref.shape
    slots = off.shape[0]
    off_part = slots // CHUNKS
    live = place_ref[0]
    me = place_ref[1]

    def off_copy(c):
        part = pl.ds(c * off_part, off_part)
        return pltpu.make_async_copy(off_hbm.at[part], off.at[part], off_sem.at[c])

    for c in range(CHUNKS):
        off_copy(c).start()

    def fill(b, carry):
        acc[b] = part_ref[b]
        return carry

    lax.fori_loop(0, blocks, fill, 0, unroll=4)

    @pl.loop(0, CHUNKS)
    def _(c):
        off_copy(c).wait()

        @pl.loop(0, off_part // GROUP)
        def _(g):
            base = c * off_part + g * GROUP

            @pl.when(base < live)
            def _():
                products = [
                    dot_nt(fetched_ref[slot_ref[base + u]], off[base + u]) for u in range(GROUP)
                ]
                for u in range(GROUP):
                    row = row_ref[base + u]
                    acc[row] = acc[row] + products[u]

    mass = row_to_column(jnp.sum(all_ref[...], axis=0), seed_cols) / vertices
    mass = jnp.broadcast_to(mass, (seed_cols, width))
    seeds = jnp.broadcast_to(seed_ref[...], (seed_cols, width)) - me * (blocks * width)
    lane = lax.broadcasted_iota(jnp.int32, (seed_cols, width), 1)
    seeds = seeds - lane

    def finish(b, carry):
        dead_mass, moved, own = carry
        here = pl.ds(pl.multiple_of(b * width, width), width)
        dead = dang_ref[pl.ds(b, 1), :].astype(jnp.float32)
        is_seed = seeds == b * width
        rank = rank_ref[:, here]
        updated = DAMP * (acc[b] + mass) + jnp.where(is_seed, 1.0 - DAMP, 0.0)
        rank_new[:, here] = updated
        if not final:
            src_out[b] = (updated * (1.0 - dead)).astype(src_out.dtype)
        return (
            dead_mass + updated * dead,
            moved + jnp.abs(updated - rank),
            own + jnp.where(is_seed, updated, 0.0),
        )

    nothing = jnp.zeros((seed_cols, width), jnp.float32)
    part = blocks // CHUNKS

    def rank_copy(c):
        here = pl.ds(c * part * width, part * width)
        return pltpu.make_async_copy(rank_new.at[:, here], rank_out.at[:, here], rank_sem.at[c])

    sums = (nothing, nothing, nothing)
    for c in range(CHUNKS):
        sums = lax.fori_loop(c * part, (c + 1) * part, finish, sums, unroll=4)
        if final:
            rank_copy(c).start()
    mass, moved, own = [jnp.sum(s, axis=1, keepdims=True) for s in sums]
    rows = columns_to_rows({0: mass, 1: own, 2 + iteration: moved}, seed_cols)
    kind = lax.broadcasted_iota(jnp.int32, rows.shape, 0)
    stat_out[...] = rows + jnp.where(kind >= 2, stat_ref[...], 0.0)
    if final:
        for c in range(CHUNKS):
            rank_copy(c).wait()


def step(vertices, iteration, slot, row, place, off, rank, part, fetched, stats, dang, seeds, stat):
    final = iteration == ITERS - 1
    blocks, seed_cols, width = part.shape
    flops = 2 * seed_cols * width * width * off.shape[0]
    rank_type = jax.ShapeDtypeStruct(rank.shape, rank.dtype)
    src_type = jax.ShapeDtypeStruct(part.shape, fetched.dtype)
    stat_type = jax.ShapeDtypeStruct(stat.shape, stat.dtype)
    return pl.pallas_call(
        functools.partial(step_kernel, vertices, iteration, final),
        out_shape=(rank_type, stat_type) if final else (rank_type, src_type, stat_type),
        in_specs=[SCALARS, SCALARS, SCALARS, FAR] + [WHOLE] * 7,
        out_specs=(FAR, WHOLE) if final else (WHOLE, WHOLE, WHOLE),
        scratch_shapes=[
            pltpu.VMEM(off.shape, off.dtype),
            pltpu.VMEM((blocks + 1, seed_cols, width), jnp.float32),
            pltpu.SemaphoreType.DMA((CHUNKS,)),
        ]
        + ([pltpu.VMEM(rank.shape, rank.dtype), pltpu.SemaphoreType.DMA((CHUNKS,))] if final else []),
        compiler_params=pltpu.CompilerParams(vmem_limit_bytes=STEP_BYTES),
        cost_estimate=pl.CostEstimate(
            flops=flops, bytes_accessed=2 * off.size, transcendentals=0
        ),
        name="power_step",
    )(slot, row, place, off, rank, part, fetched, stats, dang, seeds, stat)


def plan_requests(tile_src, tile_count, blocks, count):
    source = tile_src[0]
    live = jnp.arange(source.shape[0], dtype=jnp.int32) < tile_count[0]
    holder = source // blocks
    inside = source - holder * blocks
    held = holder[None, :] == jnp.arange(count, dtype=jnp.int32)[:, None]
    read = jnp.logical_and(held, live[None, :])
    low = jnp.min(jnp.where(read, inside[None, :], blocks - 1), axis=1)
    high = jnp.max(jnp.where(read, inside[None, :], 0), axis=1)
    tile_low = jnp.sum(jnp.where(held, low[:, None], 0), axis=0)
    slot = holder * CAP + (inside != tile_low).astype(jnp.int32)
    return jnp.stack([low, high], axis=1).reshape(-1), slot, live


def on_device(rank_in, band_tiles, off_tiles, tile_src, tile_row, tile_count, seed_ids, dangling):
    blocks = band_tiles.shape[0]
    width = band_tiles.shape[2]
    seed_cols = rank_in.shape[0]
    count = lax.axis_size("dom")
    groups = lax.axis_size("seed")
    vertices = blocks * width * count
    me = lax.axis_index("dom")

    requests, slot, live = plan_requests(tile_src, tile_count, blocks, count)
    rows = jnp.where(live, tile_row[0], blocks)
    padded = jnp.pad(requests, (0, STAT_ROWS * LANES - count * CAP)).reshape(STAT_ROWS, LANES)
    dang = dangling.reshape(blocks, width)
    asked, src, mass = first(padded.astype(jnp.float32), dang, rank_in, blocks, width, count)
    asked = asked.reshape(count, STAT_ROWS * LANES)
    wanted = lax.dynamic_slice_in_dim(asked, me * CAP, CAP, axis=1)
    wanted = wanted.astype(jnp.int32).reshape(-1)
    stat = jnp.pad(
        jnp.sum(mass, axis=1)[None, :], ((0, STAT_ROWS - 1), (0, LANES - seed_cols))
    )

    seeds = seed_ids[:, None]
    place = jnp.stack([tile_count[0], me.astype(jnp.int32)])
    rank = rank_in
    for iteration in range(ITERS):
        fetched, stats, part = exchange(wanted, src, stat, band_tiles, count)
        fetched = fetched.reshape((count * CAP,) + src.shape[1:])
        rank, *src, stat = step(
            vertices, iteration, slot, rows, place, off_tiles, rank, part, fetched, stats, dang,
            seeds, stat,
        )
        src = src[0] if src else None
    mine, whole = last(stat, count, groups)
    change = mine[2 : 2 + ITERS, :seed_cols] / vertices
    total_change = jnp.sum(whole[2 : 2 + ITERS], axis=1) / vertices / (seed_cols * groups)
    return (rank, change, total_change, mine[1, :seed_cols])


def solution(mesh):
    return jax.shard_map(
        on_device,
        mesh=mesh,
        in_specs=(
            P("seed", "dom"),
            P("dom", None, None, None),
            P("dom", None, None),
            P("dom", None),
            P("dom", None),
            P("dom"),
            P("seed"),
            P("dom"),
        ),
        out_specs=(P("seed", "dom"), P(None, "seed"), P(), P("seed")),
        check_vma=False,
    )
```
